32 devices in a mesh: gx: 8 (over y, x, core), gy: 4 (over z).
Axes of the slice: x: 2, y: 2, z: 4, core: 2. Of those that a mesh axis runs over, the one named last changes fastest.
Arguments:
- pressure: float32 [10, 512, 512], P(None, 'gx', 'gy'), may hold values from -6 to 6
- sat_old: float32 [10, 512, 512], P(None, 'gx', 'gy'), may hold values from 0.3 to 1
- soil_type: int32 [10, 512, 512], P(None, 'gx', 'gy'), may hold values from 0 to 12
- ks_table: float32 [13], replicated, may hold values from 0.1 to 2
- alpha_table: float32 [13], replicated, may hold values from 0.5 to 4
- porosity_table: float32 [13], replicated, may hold values from 0.2 to 0.5
- rain: float32 [262144], P(('gx', 'gy')), may hold values from 0 to 2
- evapo: float32 [262144], P(('gx', 'gy')), may hold values from 0 to 1
- land_mask: int32 [262144], P(('gx', 'gy')), may hold values 0 or 1
- tile: int32 [262144, 1], P(('gx', 'gy')), may hold values from 0 to 31; in each aligned block of 8192 rows (0 to 8191, 8192 to 16383, ...) at most 256 rows name the same one
- cell: int32 [262144], P(('gx', 'gy')), may hold values from 0 to 8191
- theta: float32 [10, 262144], P(None, ('gx', 'gy')), may hold values from 0.1 to 0.5
- kappa: float32 [10, 262144], P(None, ('gx', 'gy')), may hold values from 0.2 to 5
Outputs:
- pressure_next: float32 [10, 512, 512], P(None, 'gx', 'gy')
- residual_next: float32 [10, 512, 512], P(None, 'gx', 'gy')
- theta_next: float32 [10, 262144], P(None, ('gx', 'gy'))
The draws below stay inside these ranges and needn't reach their ends.
Inputs may be any that keep to these rules, and one draw needn't show every extreme that they name: Among the 8192 land columns of one device at most 256 name the same tile, and that many do in some device.
All inputs are finite; a program needn't handle non-finite values. No bound on the sum of `land_mask` on one device may be relied on, other than what follows from the above.
Results may differ from the reference program's by a relative error of at most 0.0003.
Values sent between devices are 32-bit elements; how exact they have to be, the bound alone decides.
A program may use at most 128 MiB of HBM per device.

```python
import math
import jax
import jax.numpy as jnp
import numpy as np

CX = 64
CY = 128
NZ = 10
NLEV = 10
NSOIL = 13
LAND_DEV = 8192
NX = 512
NY = 512
LANDS = 262144
CAP = 256
N_GY = 4
DEVICES = 32


def place_ends(array, own_key, smallest, largest):
    shape = array.shape
    place = [jax.random.randint(jax.random.fold_in(own_key, axis), (), 0, shape[axis]) for axis in range(len(shape))]
    array = array.at[tuple(place)].set(smallest)
    longest = shape.index(max(shape))
    place[longest] = (place[longest] + 1) % shape[longest]
    return array.at[tuple(place)].set(largest)


def block_levels(key, extent, split, least, top_value):
    def one(axis_at, shards_of):
        heights = jax.random.uniform(jax.random.fold_in(jax.random.fold_in(key, 6), axis_at), (shards_of,), jnp.float32, least / len(split), top_value / len(split))
        return jnp.repeat(jnp.exp(heights), extent[axis_at] // shards_of).reshape((-1,) + (1,) * (len(extent) - axis_at - 1))

    level = one(*split[0])
    for cut in split[1:]:
        level = level * one(*cut)
    return level


def deal_out(stream_key, own, number, rows, count, top, bound, slope):
    sequence = jax.random.permutation(stream_key, count)
    heavy_load, common = load_shares(count, rows * top, bound, slope, True), load_shares(count, rows * top, bound, slope, False)
    places = jnp.arange(count)

    def named(lengths, turn):
        used = int((lengths > 0).sum())
        fixed = max(1, used // 4)
        passed = fixed + (places - fixed + turn * (used - fixed)) % max(1, count - fixed)
        return jnp.zeros((count,), jnp.int32).at[sequence[jnp.where(places < fixed, places, passed)]].set(jnp.asarray(lengths, jnp.int32))

    lengths = jnp.where(number % 4 == 0, named(heavy_load, number // 4), named(common, number - number // 4 - 1))
    mixed = jax.random.permutation(jax.random.fold_in(own, 3), count)
    source_of, sink = mixed[0:count // 2 * 2:2], mixed[1:count // 2 * 2:2]
    room = jnp.minimum(lengths[source_of] - 1, bound - lengths[sink]) // 2
    room = jnp.where((source_of == sequence[0]) | (sink == sequence[0]) | (lengths[sink] == 0), 0, jnp.maximum(room, 0))
    passed = jax.random.randint(jax.random.fold_in(own, 4), (count // 2,), 0, 1 << 20) % (room + 1)
    lengths = lengths.at[source_of].add(-passed).at[sink].add(passed)
    members = jnp.searchsorted(jnp.cumsum(lengths), jnp.arange(rows * top), side="right").astype(jnp.int32)
    table = members.reshape(top, rows).T
    table = table[jax.random.permutation(jax.random.fold_in(own, 1), rows)]
    turn = jax.random.randint(jax.random.fold_in(own, 2), (rows, 1), 0, top)
    return jnp.take_along_axis(table, (jnp.arange(top)[None, :] + turn) % top, axis=1)


def load_shares(amount, total, bound, skew, full):
    loads = [(1 << 20) // math.isqrt(rank ** skew) + 1 for rank in range(1, amount + 1)]
    largest = bound if full else min(bound, max(-(-total // amount), total * loads[0] // sum(loads)))
    least = 1 if total - largest >= amount - 1 else 0
    holding, spare = [largest] + [least] * (amount - 1), total - largest - least * (amount - 1)
    while spare > 0:
        candidates = [i for i in range(1, amount) if holding[i] < largest] or [i for i in range(1, amount) if holding[i] < bound]
        pool, remaining = sum([loads[i] for i in candidates]), spare
        for i in candidates:
            addition = min(bound - holding[i], max(1, remaining * loads[i] // pool), spare)
            holding[i] = holding[i] + addition
            spare = spare - addition
    return np.array(holding)


def noise(key, shape, scale, reach, cuts=(), dtype=jnp.bfloat16):
    values = scale * jax.random.normal(key, shape, jnp.float32)
    if cuts:
        values = values * block_levels(key, shape, cuts, -0.22, 0.18)
    return jnp.clip(values, -reach, reach).astype(dtype)


def setup_inputs(seed: int = 0) -> dict:
    splits = jax.random.split(jax.random.key(seed), 14)
    pressure = noise(splits[0], (NZ, NX, NY), 1.0, 6.0, ((1, 8), (2, 4)), jnp.float32)
    sat_old = jnp.clip(0.3 + 0.7 * jax.random.uniform(splits[1], (NZ, NX, NY), jnp.float32) ** block_levels(splits[1], (NZ, NX, NY), ((1, 8), (2, 4)), -0.2, 0.2), 0.3, 1.0)
    soil_type = place_ends(jax.random.randint(splits[2], (NZ, NX, NY), 0, NSOIL), jax.random.fold_in(splits[2], 1), 0, NSOIL - 1).astype(jnp.int32)
    ks_table = jnp.clip(jnp.exp(jax.random.uniform(splits[3], (NSOIL,), jnp.float32, math.log(0.1), math.log(2.0))), 0.1, 2.0)
    alpha_table = jnp.clip(jnp.exp(jax.random.uniform(splits[4], (NSOIL,), jnp.float32, math.log(0.5), math.log(4.0))), 0.5, 4.0)
    porosity_table = jnp.clip(jax.random.uniform(splits[5], (NSOIL,), jnp.float32, 0.2, 0.5), 0.2, 0.5)
    rain = jnp.clip(2.0 * jax.random.uniform(splits[6], (LANDS,), jnp.float32) ** block_levels(splits[6], (LANDS,), ((0, 32),), -0.2, 0.2), 0.0, 2.0)
    evapo = jnp.clip(1.0 * jax.random.uniform(splits[7], (LANDS,), jnp.float32) ** block_levels(splits[7], (LANDS,), ((0, 32),), -0.2, 0.2), 0.0, 1.0)
    land_mask = place_ends((jax.random.randint(splits[8], (LANDS,), 0, 4) < 3).astype(jnp.int32), jax.random.fold_in(splits[8], 1), 0, 1)
    tile_keys = jax.random.split(jax.random.fold_in(splits[9], 1), LANDS // LAND_DEV)
    tile_turns = jax.random.permutation(jax.random.fold_in(splits[9], 3), LANDS // LAND_DEV)
    tile = jax.vmap(lambda own, number: deal_out(jax.random.fold_in(splits[9], 2), own, number, LAND_DEV, DEVICES, 1, CAP, 2))(tile_keys, tile_turns).reshape((LANDS, 1))
    cell = place_ends(jax.random.randint(splits[10], (LANDS,), 0, CX * CY), jax.random.fold_in(splits[10], 1), 0, (CX * CY) - 1).astype(jnp.int32)
    theta = jnp.clip(0.1 + 0.4 * jax.random.uniform(splits[11], (NLEV, LANDS), jnp.float32) ** block_levels(splits[11], (NLEV, LANDS), ((1, 32),), -0.2, 0.2), 0.1, 0.5)
    kappa = jnp.clip(jnp.exp(math.log(5.0) - 3.218876 * jax.random.uniform(splits[12], (NLEV, LANDS), jnp.float32) ** block_levels(splits[12], (NLEV, LANDS), ((1, 32),), -0.2, 0.2)), 0.2, 5.0)
    return dict(pressure=pressure, sat_old=sat_old, soil_type=soil_type, ks_table=ks_table, alpha_table=alpha_table, porosity_table=porosity_table, rain=rain, evapo=evapo, land_mask=land_mask, tile=tile, cell=cell, theta=theta, kappa=kappa)


def relperm(p, alpha):
    head = alpha * jnp.maximum(-p, 0.0)
    return 1.0 / (1.0 + head * head)

def mean_face(first, second):
    total = first + second
    return jnp.where(first * second > 0, 2.0 * first * second / jnp.where(total > 0, total, 1.0), 0.0)

def residual_core(padp, padk, pada, sat_old, phi, source):
    width_a = padp.shape[1] - 2
    width_b = padp.shape[2] - 2
    krel = relperm(padp, pada)
    p_mid = padp[:, 1:-1, 1:-1]
    k_mid = padk[:, 1:-1, 1:-1]
    r_mid = krel[:, 1:-1, 1:-1]
    outflow = jnp.zeros_like(p_mid)
    for sx, sy in ((0, 1), (2, 1), (1, 0), (1, 2)):
        p_nb = padp[:, sx:sx + width_a, sy:sy + width_b]
        k_nb = padk[:, sx:sx + width_a, sy:sy + width_b]
        r_nb = krel[:, sx:sx + width_a, sy:sy + width_b]
        outflow = outflow + mean_face(k_mid, k_nb) * 0.5 * (r_mid + r_nb) * (p_mid - p_nb)
    down = mean_face(k_mid[:-1], k_mid[1:]) * 0.5 * (r_mid[:-1] + r_mid[1:]) * (p_mid[:-1] - p_mid[1:] + 1.0)
    outflow = outflow + jnp.pad(down, ((0, 1), (0, 0), (0, 0))) - jnp.pad(down, ((1, 0), (0, 0), (0, 0)))
    return phi * (jnp.sqrt(r_mid) - sat_old) + 0.5 * outflow - 0.5 * source

def soil_solve(theta, kappa, p_top, s_top):
    levels = theta.shape[0]
    coeff = kappa * (0.5 + s_top)[None, :]
    upper_list = []
    value_list = []
    for level in range(levels):
        below = coeff[level + 1] if level + 1 < levels else jnp.zeros_like(coeff[0])
        diag = 1.0 + coeff[level] + below
        rhs = theta[level] + coeff[0] * p_top if level == 0 else theta[level]
        if level == 0:
            denom = diag
            value = rhs / denom
        else:
            denom = diag + coeff[level] * upper_list[-1]
            value = (rhs + coeff[level] * value_list[-1]) / denom
        upper_list.append(-below / denom)
        value_list.append(value)
    result = [value_list[-1]]
    for level in range(levels - 2, -1, -1):
        result.append(value_list[level] - upper_list[level] * result[-1])
    return jnp.stack(result[::-1])

def reference(pressure, sat_old, soil_type, ks_table, alpha_table, porosity_table, rain, evapo, land_mask, tile, cell, theta, kappa):
    depth, size_x, size_y = pressure.shape
    ks = jnp.take(ks_table, soil_type)
    alpha = jnp.take(alpha_table, soil_type)
    phi = jnp.take(porosity_table, soil_type)
    target = tile[:, 0]
    pos_x = target // N_GY * CX + cell // CY
    pos_y = target % N_GY * CY + cell % CY
    flat = (pos_x * size_y + pos_y).astype(jnp.int32)
    live = land_mask.astype(jnp.float32)
    maps = jnp.zeros((2, size_x * size_y), jnp.float32).at[:, flat].add(jnp.stack([live * rain, live * evapo]))
    maps = maps.reshape(2, size_x, size_y)
    decay = jnp.exp(-jnp.arange(depth).astype(jnp.float32) / 2.0)
    rootfrac = decay / jnp.sum(decay)
    top = (jnp.arange(depth) == 0).astype(jnp.float32)
    source = top[:, None, None] * maps[0][None] - rootfrac[:, None, None] * maps[1][None]
    edge = ((0, 0), (1, 1), (1, 1))
    padk = jnp.pad(ks, edge)
    pada = jnp.pad(alpha, edge)
    first = residual_core(jnp.pad(pressure, edge), padk, pada, sat_old, phi, source)
    pressure_next = pressure - 0.8 * first
    residual_next = residual_core(jnp.pad(pressure_next, edge), padk, pada, sat_old, phi, source)
    p_top = pressure_next[0].reshape(-1)[flat]
    s_top = jnp.sqrt(relperm(pressure_next[0], alpha[0])).reshape(-1)[flat]
    solved = soil_solve(theta, kappa, p_top, s_top)
    theta_next = jnp.where(land_mask[None, :] == 1, solved, theta)
    return (pressure_next, residual_next, theta_next)
```

```python
import functools
import math

import jax
import jax.numpy as jnp
from jax import lax
from jax.experimental import pallas as pl
from jax.experimental.pallas import tpu as pltpu
from jax.sharding import PartitionSpec as P

F32 = jnp.float32
BF16 = jnp.bfloat16
MESH = pl.DeviceIdType.MESH
NT = (((1,), (1,)), ((), ()))
NN = (((1,), (0,)), ((), ()))
GROUP = 8


def dot(a, b, dims):
    return lax.dot_general(a, b, dims, preferred_element_type=F32)


def halves(value):
    high = value.astype(BF16).astype(F32)
    return high, value - high


def relperm(p, alpha):
    head = alpha * jnp.maximum(-p, 0.0)
    return 1.0 / (1.0 + head * head)


def half_mean(first, second):
    product = first * second
    total = first + second
    return jnp.where(product > 0, product / jnp.where(total > 0, total, 1.0), 0.0)


def iota(shape, dim):
    return lax.broadcasted_iota(jnp.int32, shape, dim)


def kernel(
    dims,
    ks_t, al_t, po_t,
    press, sat_old, soil, rain, evapo, mask, tile, cell, theta, kappa,
    p_out, r_out, t_out,
    onehot, acc, send, recv, ans, ret, rank_s,
    ks, al, phi, kr, gx, gy, gz, base, krn, oney, macc,
    own_x, halo_x, own_y, halo_y, own2_x, halo2_x, own2_y, halo2_y, gbx, gby, fbx, fby,
    th_s, ka_s, so_s, top_s,
    send1, recv1, send2, recv2, hs1, hr1, hs2, hr2,
):
    count_x, count_y, slots = dims
    peers = count_x * count_y
    depth, size_x, size_y = press.shape
    levels, land = theta.shape
    rows = land // 128
    parts = slots // 128
    classes = ks_t.shape[0]
    my_x = lax.axis_index("gx")
    my_y = lax.axis_index("gy")
    me = my_x * count_y + my_y

    for ref in (own_x, halo_x, own_y, halo_y, own2_x, halo2_x, own2_y, halo2_y):
        ref[...] = jnp.zeros_like(ref)

    barrier = pltpu.get_barrier_semaphore()

    def greet(i, carry):
        other = lax.rem(me + i, peers)
        pl.semaphore_signal(
            barrier, inc=1, device_id=(other // count_y, lax.rem(other, count_y)), device_id_type=MESH
        )
        return carry

    lax.fori_loop(1, peers, greet, 0)

    row_id = iota((size_x, size_y), 0)
    lane_id = iota((size_x, size_y), 1)

    def properties(z, carry):
        low, high = carry
        kind = soil[z]
        k = jnp.zeros((size_x, size_y), F32)
        a = k
        f = k
        for c in range(classes):
            hit = kind == c
            k = jnp.where(hit, ks_t[c], k)
            a = jnp.where(hit, al_t[c], a)
            f = jnp.where(hit, po_t[c], f)
        p = press[z]
        r = relperm(p, a)
        ks[z] = k
        al[z] = a
        phi[z] = f
        kr[z] = r
        for n, value in enumerate((p, k, r)):
            own_x[0, pl.ds(n * 16 + z, 1), :] = value[:1, :]
            own_x[1, pl.ds(n * 16 + z, 1), :] = value[size_x - 1 :, :]
            here = lane_id == n * 32 + z
            low = jnp.where(here, value[:, :1], low)
            high = jnp.where(here, value[:, size_y - 1 :], high)
        return low, high

    blank = jnp.zeros((size_x, size_y), F32)
    low, high = lax.fori_loop(0, depth, properties, (blank, blank))
    own_y[0] = low
    own_y[1] = high

    pl.semaphore_wait(barrier, peers - 1)

    def sides(src_x, dst_x, src_y, dst_y, sems_s, sems_r):
        plan = (
            (my_x > 0, src_x, dst_x, 0, my_x - 1, my_y),
            (my_x < count_x - 1, src_x, dst_x, 1, my_x + 1, my_y),
            (my_y > 0, src_y, dst_y, 0, my_x, my_y - 1),
            (my_y < count_y - 1, src_y, dst_y, 1, my_x, my_y + 1),
        )
        made = []
        for n, (there, src, dst, side, at_x, at_y) in enumerate(plan):
            mate = n - side + 1 - side
            outward = pltpu.make_async_remote_copy(
                src_ref=src.at[side], dst_ref=dst.at[1 - side],
                send_sem=sems_s.at[n], recv_sem=sems_r.at[mate],
                device_id=(at_x, at_y), device_id_type=MESH,
            )
            inward = pltpu.make_async_remote_copy(
                src_ref=src.at[side], dst_ref=dst.at[side],
                send_sem=sems_s.at[n], recv_sem=sems_r.at[n],
                device_id=(at_x, at_y), device_id_type=MESH,
            )
            made.append((there, outward, inward))
        return made

    first_sides = sides(own_x, halo_x, own_y, halo_y, hs1, hr1)
    for there, outward, _ in first_sides:
        pl.when(there)(outward.start)

    wide = iota((128, 256), 1)
    tall = iota((128, 256), 0)
    before = ((wide >= 128) | (tall < wide)).astype(F32).astype(BF16)
    peer_id = iota((peers, 128), 0)
    slot_id = iota((slots, 128), 0).astype(F32)
    acc[...] = jnp.zeros_like(acc)

    def dispatch(c, count):
        at = pl.ds(pl.multiple_of(c * GROUP, GROUP), GROUP)
        lanes = pl.ds(pl.multiple_of(c * GROUP * 128, 128), GROUP * 128)
        named = tile[at, :]
        live = mask[at, :].astype(F32)
        where_to = cell[at, :].astype(F32)
        cell_x = jnp.floor(where_to * (1.0 / size_y)) * size_y
        values = (
            *halves(live * rain[at, :]), *halves(live * evapo[at, :]), cell_x, where_to - cell_x
        )
        hits = [named[i : i + 1, :] == peer_id for i in range(GROUP)]
        ones = [jnp.where(h, 1.0, 0.0) for h in hits]
        sums = dot(jnp.concatenate(ones, axis=0).astype(BF16), before, NN)
        ranks = []
        for i in range(GROUP):
            part = sums[i * peers : (i + 1) * peers]
            ranks.append(jnp.sum(ones[i] * (part[:, :128] + count), axis=0, keepdims=True))
            count = count + part[:, 128:]
        rank_s[at, :] = jnp.concatenate(ranks, axis=0)
        chosen = jnp.concatenate(
            [jnp.where(r == slot_id, 1.0, 0.0).astype(BF16) for r in ranks], axis=1
        )
        onehot[:, lanes] = chosen
        left = jnp.concatenate(
            [
                jnp.concatenate(
                    [jnp.where(hits[i], v[i : i + 1, :], 0.0) for i in range(GROUP)], axis=1
                ).astype(BF16)
                for v in values
            ],
            axis=0,
        )
        acc[...] += dot(left, chosen, NT)
        return count

    lax.fori_loop(0, rows // GROUP, dispatch, jnp.zeros((peers, 128), F32))
    for v in range(3):
        full = acc[2 * v * peers : (2 * v + 1) * peers] + acc[(2 * v + 1) * peers : (2 * v + 2) * peers]
        for h in range(parts):
            send[pl.ds(v * parts + h, peers, stride=8), :] = full[:, h * 128 : (h + 1) * 128]

    def block(ref, t):
        return ref.at[pl.ds(pl.multiple_of(t * 8, 8), 8)]

    def carry_over(src, dst, sems_s, sems_r, other, landing):
        return pltpu.make_async_remote_copy(
            src_ref=block(src, other), dst_ref=block(dst, landing),
            send_sem=sems_s.at[other], recv_sem=sems_r.at[landing],
            device_id=(other // count_y, lax.rem(other, count_y)), device_id_type=MESH,
        )

    def exchange(src, dst, sems_s, sems_r):
        def step(i, carry):
            other = lax.rem(me + i, peers)
            carry_over(src, dst, sems_s, sems_r, other, me).start()
            return carry

        lax.fori_loop(1, peers, step, 0)
        mine = pl.ds(pl.multiple_of(me * 8, 8), 8)
        dst[mine, :] = src[mine, :]

    def arrive(src, dst, sems_s, sems_r):
        def step(i, carry):
            other = lax.rem(me + i, peers)
            carry_over(src, dst, sems_s, sems_r, other, other).wait_recv()
            return carry

        lax.fori_loop(1, peers, step, 0)

    def sent(src, dst, sems_s, sems_r):
        def step(i, carry):
            other = lax.rem(me + i, peers)
            carry_over(src, dst, sems_s, sems_r, other, me).wait_send()
            return carry

        lax.fori_loop(1, peers, step, 0)

    exchange(send, recv, send1, recv1)

    def spread(j, carry):
        lanes = pl.ds(pl.multiple_of(j * 128, 128), 128)
        for src, dst in ((theta, th_s), (kappa, ka_s)):
            for k in range(levels):
                dst[k, pl.ds(j, 1), :] = src[k : k + 1, lanes]
        return carry

    lax.fori_loop(0, rows, spread, 0)

    def outflow(z, before_z, pr, rel):
        p = pr[z]
        r = rel[z]
        zn = jnp.minimum(z + 1, depth - 1)
        fx = gx[z] * (r + pltpu.roll(r, 1, 0)) * (p - pltpu.roll(p, 1, 0))
        fy = gy[z] * (r + pltpu.roll(r, 1, 1)) * (p - pltpu.roll(p, 1, 1))
        down = gz[z] * (r + rel[zn]) * (p - pr[zn] + 1.0)
        total = (
            fx - pltpu.roll(fx, size_x - 1, 0) + fy - pltpu.roll(fy, size_y - 1, 1) + down - before_z
        )
        return total, down

    def boundary(z):
        total = jnp.where(row_id == 0, fbx[0, pl.ds(z, 1), :], 0.0)
        total = jnp.where(row_id == size_x - 1, fbx[1, pl.ds(z, 1), :], total)
        one = pltpu.roll(fby[0], lax.rem(size_y - z, size_y), 1)
        two = pltpu.roll(fby[1], size_y - 1 - z, 1)
        return total + jnp.where(lane_id == 0, one, 0.0) + jnp.where(lane_id == size_y - 1, two, 0.0)

    def faces(z, carry):
        k = ks[z]
        zn = jnp.minimum(z + 1, depth - 1)
        gx[z] = jnp.where(row_id == 0, 0.0, half_mean(k, pltpu.roll(k, 1, 0)))
        gy[z] = jnp.where(lane_id == 0, 0.0, half_mean(k, pltpu.roll(k, 1, 1)))
        gz[z] = jnp.where(z < depth - 1, half_mean(k, ks[zn]), 0.0)
        total, down = outflow(z, carry, press, kr)
        base[z] = press[z] - 0.8 * (phi[z] * (jnp.sqrt(kr[z]) - sat_old[z]) + 0.5 * total)
        return down

    lax.fori_loop(0, depth, faces, blank)

    for there, _, inward in first_sides:
        pl.when(there)(inward.wait_recv)
    for s in range(2):
        mine, other = own_x[s], halo_x[s]
        gbx[s] = half_mean(mine[16:32], other[16:32])
        fbx[s] = gbx[s] * (mine[32:48] + other[32:48]) * (mine[0:16] - other[0:16])
        mine, other = own_y[s], halo_y[s]
        gby[s] = half_mean(pltpu.roll(mine, size_y - 32, 1), pltpu.roll(other, size_y - 32, 1))
        fby[s] = gby[s] * pltpu.roll(mine + other, size_y - 64, 1) * (mine - other)

    arrive(send, recv, send1, recv1)
    macc[...] = jnp.zeros_like(macc)
    x_id = iota((size_x, 128), 0).astype(F32)
    y_id = iota((size_y, 128), 0).astype(F32)
    srcs = GROUP // parts

    def gather_in(c, carry):
        lanes = pl.ds(pl.multiple_of(c * GROUP * 128, 128), GROUP * 128)
        left = [[] for _ in range(4)]
        right = []
        for i in range(srcs):
            got = recv[pl.ds(pl.multiple_of((c * srcs + i) * 8, 8), 8), :]
            high_v, low_v = halves(got)
            at_x = jnp.floor(got * (1.0 / size_y))
            at_y = got - at_x * size_y
            for h in range(parts):
                n = 2 * parts + h
                hit = at_x[n : n + 1, :] == x_id
                right.append(jnp.where(at_y[n : n + 1, :] == y_id, 1.0, 0.0).astype(BF16))
                for v in range(2):
                    m = v * parts + h
                    left[2 * v].append(jnp.where(hit, high_v[m : m + 1, :], 0.0).astype(BF16))
                    left[2 * v + 1].append(jnp.where(hit, low_v[m : m + 1, :], 0.0).astype(BF16))
        right = jnp.concatenate(right, axis=1)
        oney[:, lanes] = right
        left = jnp.concatenate([jnp.concatenate(l, axis=1) for l in left], axis=0)
        macc[...] += dot(left, right, NT)
        return carry

    lax.fori_loop(0, peers * parts // GROUP, gather_in, 0)
    rain_map = macc[0:size_x] + macc[size_x : 2 * size_x]
    et_map = macc[2 * size_x : 3 * size_x] + macc[3 * size_x : 4 * size_x]

    scale = 1.0 / sum(math.exp(-z / 2.0) for z in range(depth))

    def update(z, carry):
        frac, low, high = carry
        source = jnp.where(z == 0, rain_map, 0.0) - frac * et_map
        p = base[z] - 0.4 * boundary(z) + 0.4 * source
        r = relperm(p, al[z])
        p_out[z] = p
        krn[z] = r
        for n, value in enumerate((p, r)):
            own2_x[0, pl.ds(n * 16 + z, 1), :] = value[:1, :]
            own2_x[1, pl.ds(n * 16 + z, 1), :] = value[size_x - 1 :, :]
            here = lane_id == n * 32 + z
            low = jnp.where(here, value[:, :1], low)
            high = jnp.where(here, value[:, size_y - 1 :], high)
        return frac * math.exp(-0.5), low, high

    _, low, high = lax.fori_loop(0, depth, update, (jnp.float32(scale), blank, blank))
    own2_y[0] = low
    own2_y[1] = high
    second_sides = sides(own2_x, halo2_x, own2_y, halo2_y, hs2, hr2)
    for there, outward, _ in second_sides:
        pl.when(there)(outward.start)

    fields = []
    for field in (p_out[0], jnp.sqrt(krn[0])):
        high_v, low_v = halves(field)
        fields.append(jnp.concatenate([high_v, low_v], axis=1))
    top_s[...] = jnp.concatenate(fields, axis=0).astype(BF16)

    def answer(c, carry):
        lanes = pl.ds(pl.multiple_of(c * GROUP * 128, 128), GROUP * 128)
        right = oney[:, lanes]
        picked = dot(top_s[...], jnp.concatenate([right, right], axis=0), NN)
        for i in range(srcs):
            at = pl.ds(pl.multiple_of((c * srcs + i) * 8, 8), 8)
            at_x = jnp.floor(recv[at, :] * (1.0 / size_y))
            out = [None] * (2 * parts)
            for h in range(parts):
                n = 2 * parts + h
                hit = at_x[n : n + 1, :] == x_id
                j = (i * parts + h) * 128
                for v in range(2):
                    out[v * parts + h] = jnp.sum(
                        jnp.where(hit, picked[v * size_x : (v + 1) * size_x, j : j + 128], 0.0),
                        axis=0, keepdims=True,
                    )
            out.append(jnp.zeros((8 - 2 * parts, 128), F32))
            ans[at, :] = jnp.concatenate(out, axis=0)
        return carry

    lax.fori_loop(0, peers * parts // GROUP, answer, 0)
    exchange(ans, ret, send2, recv2)

    for there, _, inward in second_sides:
        pl.when(there)(inward.wait_recv)
    for s in range(2):
        mine, other = own2_x[s], halo2_x[s]
        fbx[s] = gbx[s] * (mine[16:32] + other[16:32]) * (mine[0:16] - other[0:16])
        mine, other = own2_y[s], halo2_y[s]
        fby[s] = gby[s] * pltpu.roll(mine + other, size_y - 32, 1) * (mine - other)

    def residual(z, carry):
        frac, previous = carry
        total, down = outflow(z, previous, p_out, krn)
        source = jnp.where(z == 0, rain_map, 0.0) - frac * et_map
        r_out[z] = phi[z] * (jnp.sqrt(krn[z]) - sat_old[z]) + 0.5 * (total + boundary(z)) - 0.5 * source
        return frac * math.exp(-0.5), down

    lax.fori_loop(0, depth, residual, (jnp.float32(scale), blank))

    arrive(ans, ret, send2, recv2)
    tops = []
    for v in range(2):
        value = jnp.concatenate(
            [ret[pl.ds(v * parts + h, peers, stride=8), :] for h in range(parts)], axis=1
        )
        tops.extend(halves(value))
    tops = jnp.concatenate(tops, axis=0).astype(BF16)

    def solve(c, carry):
        at = pl.ds(pl.multiple_of(c * GROUP, GROUP), GROUP)
        lanes = pl.ds(pl.multiple_of(c * GROUP * 128, 128), GROUP * 128)
        named = tile[at, :]
        picked = dot(tops, onehot[:, lanes], NN)
        both = []
        for v in range(2):
            value = picked[2 * v * peers : (2 * v + 1) * peers]
            value = value + picked[(2 * v + 1) * peers : (2 * v + 2) * peers]
            both.append(
                jnp.concatenate(
                    [
                        jnp.sum(
                            jnp.where(
                                named[i : i + 1, :] == peer_id, value[:, i * 128 : (i + 1) * 128], 0.0
                            ),
                            axis=0, keepdims=True,
                        )
                        for i in range(GROUP)
                    ],
                    axis=0,
                )
            )
        p_top, s_top = both
        active = mask[at, :] == 1
        coeff = [ka_s[k, at, :] * (0.5 + s_top) for k in range(levels)]
        coeff.append(jnp.zeros_like(p_top))
        upper, value = [], []
        for k in range(levels):
            diag = 1.0 + coeff[k] + coeff[k + 1]
            right = th_s[k, at, :]
            if k == 0:
                right = right + coeff[0] * p_top
            else:
                diag = diag - coeff[k] * upper[-1]
                right = right + coeff[k] * value[-1]
            inverse = 1.0 / diag
            upper.append(coeff[k + 1] * inverse)
            value.append(right * inverse)
        result = value[-1]
        so_s[levels - 1, at, :] = jnp.where(active, result, th_s[levels - 1, at, :])
        for k in range(levels - 2, -1, -1):
            result = value[k] + upper[k] * result
            so_s[k, at, :] = jnp.where(active, result, th_s[k, at, :])
        return carry

    lax.fori_loop(0, rows // GROUP, solve, 0)

    def collect(j, carry):
        lanes = pl.ds(pl.multiple_of(j * 128, 128), 128)
        for k in range(levels):
            t_out[k : k + 1, lanes] = so_s[k, pl.ds(j, 1), :]
        return carry

    lax.fori_loop(0, rows, collect, 0)

    sent(send, recv, send1, recv1)
    sent(ans, ret, send2, recv2)
    for made in (first_sides, second_sides):
        for there, outward, _ in made:
            pl.when(there)(outward.wait_send)


def local(dims, pressure, sat_old, soil_type, ks_table, alpha_table, porosity_table,
          rain, evapo, land_mask, tile, cell, theta, kappa):
    count_x, count_y = dims
    peers = count_x * count_y
    depth, size_x, size_y = pressure.shape
    levels, land = theta.shape
    slots = land // 32
    rows = land // 128
    flat = lambda value: value.reshape(rows, 128)
    grid = pltpu.VMEM((depth, size_x, size_y), F32)
    column = pltpu.VMEM((levels, rows, 128), F32)
    message = pltpu.VMEM((peers * 8, 128), F32)
    dma = pltpu.SemaphoreType.DMA
    vmem = pl.BlockSpec(memory_space=pltpu.VMEM)
    smem = pl.BlockSpec(memory_space=pltpu.SMEM)
    edge_x = pltpu.VMEM((2, 48, size_y), F32)
    edge2_x = pltpu.VMEM((2, 32, size_y), F32)
    edge_y = pltpu.VMEM((2, size_x, size_y), F32)
    rows_x = pltpu.VMEM((2, 16, size_y), F32)
    return pl.pallas_call(
        functools.partial(kernel, (count_x, count_y, slots)),
        out_shape=(
            jax.ShapeDtypeStruct(pressure.shape, F32),
            jax.ShapeDtypeStruct(pressure.shape, F32),
            jax.ShapeDtypeStruct(theta.shape, F32),
        ),
        in_specs=[smem] * 3 + [vmem] * 10,
        out_specs=(vmem, vmem, vmem),
        scratch_shapes=[
            pltpu.VMEM((slots, land), BF16),
            pltpu.VMEM((6 * peers, slots), F32),
            message, message, message, message,
            pltpu.VMEM((rows, 128), F32),
            grid, grid, grid, grid, grid, grid, grid, grid, grid,
            pltpu.VMEM((size_y, peers * slots), BF16),
            pltpu.VMEM((4 * size_x, size_y), F32),
            edge_x, edge_x, edge_y, edge_y, edge2_x, edge2_x, edge_y, edge_y,
            rows_x, edge_y, rows_x, edge_y,
            column, column, column,
            pltpu.VMEM((2 * size_x, 2 * size_y), BF16),
            dma((peers,)), dma((peers,)), dma((peers,)), dma((peers,)),
            dma((4,)), dma((4,)), dma((4,)), dma((4,)),
        ],
        compiler_params=pltpu.CompilerParams(
            collective_id=0, has_side_effects=True, vmem_limit_bytes=50 * 1024 * 1024
        ),
    )(
        ks_table, alpha_table, porosity_table, pressure, sat_old, soil_type,
        flat(rain), flat(evapo), flat(land_mask), flat(tile), flat(cell), theta, kappa,
    )


def solution(mesh):
    in_specs = (
        P(None, "gx", "gy"),
        P(None, "gx", "gy"),
        P(None, "gx", "gy"),
        P(),
        P(),
        P(),
        P(("gx", "gy")),
        P(("gx", "gy")),
        P(("gx", "gy")),
        P(("gx", "gy"), None),
        P(("gx", "gy")),
        P(None, ("gx", "gy")),
        P(None, ("gx", "gy")),
    )
    out_specs = (P(None, "gx", "gy"), P(None, "gx", "gy"), P(None, ("gx", "gy")))
    dims = (mesh.shape["gx"], mesh.shape["gy"])
    return jax.shard_map(
        functools.partial(local, dims), mesh=mesh, in_specs=in_specs, out_specs=out_specs, check_vma=False
    )
```

```python
import functools
import math

import jax
import jax.numpy as jnp
from jax import lax
from jax.experimental import pallas as pl
from jax.experimental.pallas import tpu as pltpu
from jax.sharding import PartitionSpec as P

F32 = jnp.float32
BF16 = jnp.bfloat16
MESH = pl.DeviceIdType.MESH
NT = (((1,), (1,)), ((), ()))
NN = (((1,), (0,)), ((), ()))
GROUP = 8


def dot(a, b, dims):
    return lax.dot_general(a, b, dims, preferred_element_type=F32)


def halves(value):
    high = value.astype(BF16).astype(F32)
    return high, value - high


def relperm(p, alpha):
    head = alpha * jnp.maximum(-p, 0.0)
    return 1.0 / (1.0 + head * head)


def half_mean(first, second):
    product = first * second
    total = first + second
    return jnp.where(product > 0, product / jnp.where(total > 0, total, 1.0), 0.0)


def wide_row(row, count):
    return jnp.concatenate([jnp.broadcast_to(row, (16, 128)).astype(BF16)] * (count // 16), axis=0)


def iota16(count):
    return lax.broadcasted_iota(jnp.int32, (count, 128), 0).astype(F32).astype(BF16)


def iota(shape, dim):
    return lax.broadcasted_iota(jnp.int32, shape, dim)


def kernel(
    dims,
    *refs,
):
    given, refs = refs[:13], refs[13:]
    (p_out, r_out, t_out), refs = refs[:3], refs[3:]
    held, refs = refs[:13], refs[13:]
    (ks_t, al_t, po_t, press, sat_old, soil, rain, evapo, mask, tile, cell, theta, kappa) = held
    (
        onehot, acc, send, recv, ans, ret,
        ks, al, phi, kr, gx, gy, gz, base, krn, oney, macc,
        own_x, halo_x, own_y, halo_y, own2_x, halo2_x, own2_y, halo2_y, gbx, gby, fbx, fby,
        th_s, ka_s, so_s, top_s, found,
        send1, recv1, send2, recv2, hs1, hr1, hs2, hr2, loaded,
    ) = refs
    loads = [
        pltpu.make_async_copy(src, dst, loaded.at[n]) for n, (src, dst) in enumerate(zip(given, held))
    ]
    for n in (9, 8, 10, 6, 7, 5, 0, 1, 2, 3, 4, 11, 12):
        loads[n].start()

    count_x, count_y, slots = dims
    peers = count_x * count_y
    depth, size_x, size_y = press.shape
    levels, land = theta.shape
    rows = land // 128
    parts = slots // 128
    classes = ks_t.shape[0]
    my_x = lax.axis_index("gx")
    my_y = lax.axis_index("gy")
    me = my_x * count_y + my_y

    for ref in (own_x, halo_x, own_y, halo_y, own2_x, halo2_x, own2_y, halo2_y):
        ref[...] = jnp.zeros_like(ref)

    barrier = pltpu.get_barrier_semaphore()

    def greet(i, carry):
        other = lax.rem(me + i, peers)
        pl.semaphore_signal(
            barrier, inc=1, device_id=(other // count_y, lax.rem(other, count_y)), device_id_type=MESH
        )
        return carry

    lax.fori_loop(1, peers, greet, 0)

    row_id = iota((size_x, size_y), 0)
    lane_id = iota((size_x, size_y), 1)

    wide = iota((128, 256), 1)
    tall = iota((128, 256), 0)
    before = ((wide >= 128) | (tall < wide)).astype(F32).astype(BF16)
    peer_id = iota((peers, 128), 0).astype(F32)
    peer16 = iota16(peers)
    slot16 = iota16(slots)
    acc[...] = jnp.zeros_like(acc)
    for n in (9, 8, 10, 6, 7):
        loads[n].wait()

    def dispatch(c, count):
        at = pl.ds(pl.multiple_of(c * GROUP, GROUP), GROUP)
        lanes = pl.ds(pl.multiple_of(c * GROUP * 128, 128), GROUP * 128)
        named = tile[at, :]
        live = mask[at, :].astype(F32)
        where_to = cell[at, :].astype(F32)
        cell_x = jnp.floor(where_to * (1.0 / size_y)) * size_y
        values = (
            *halves(live * rain[at, :]), *halves(live * evapo[at, :]), cell_x, where_to - cell_x
        )
        label = named.astype(F32)
        hits = [label[i : i + 1, :] == peer_id for i in range(GROUP)]
        hits16 = [wide_row(label[i : i + 1, :], peers) == peer16 for i in range(GROUP)]
        one = jnp.ones((peers, 128), BF16)
        sums = dot(
            jnp.concatenate([jnp.where(h, one, jnp.zeros_like(one)) for h in hits16], axis=0), before, NN
        )
        ranks = []
        for i in range(GROUP):
            part = sums[i * peers : (i + 1) * peers]
            ranks.append(
                jnp.sum(jnp.where(hits[i], part[:, :128] + count, 0.0), axis=0, keepdims=True)
            )
            count = count + part[:, 128:]
        one = jnp.ones((slots, 128), BF16)
        chosen = jnp.concatenate(
            [jnp.where(wide_row(r, slots) == slot16, one, jnp.zeros_like(one)) for r in ranks], axis=1
        )
        onehot[:, lanes] = chosen
        nothing = jnp.zeros((peers, 128), BF16)
        left = jnp.concatenate(
            [
                jnp.concatenate(
                    [
                        jnp.where(hits16[i], wide_row(v[i : i + 1, :], peers), nothing)
                        for i in range(GROUP)
                    ],
                    axis=1,
                )
                for v in values
            ],
            axis=0,
        )
        acc[...] += dot(left, chosen, NT)
        return count

    lax.fori_loop(0, rows // GROUP, dispatch, jnp.zeros((peers, 128), F32), unroll=4)
    for v in range(3):
        full = acc[2 * v * peers : (2 * v + 1) * peers] + acc[(2 * v + 1) * peers : (2 * v + 2) * peers]
        for h in range(parts):
            send[pl.ds(v * parts + h, peers, stride=8), :] = full[:, h * 128 : (h + 1) * 128]

    def block(ref, t):
        return ref.at[pl.ds(pl.multiple_of(t * 8, 8), 8)]

    def carry_over(src, dst, sems_s, sems_r, other, landing):
        return pltpu.make_async_remote_copy(
            src_ref=block(src, other), dst_ref=block(dst, landing),
            send_sem=sems_s.at[other], recv_sem=sems_r.at[landing],
            device_id=(other // count_y, lax.rem(other, count_y)), device_id_type=MESH,
        )

    def exchange(src, dst, sems_s, sems_r):
        def step(i, carry):
            other = lax.rem(me + i, peers)
            carry_over(src, dst, sems_s, sems_r, other, me).start()
            return carry

        lax.fori_loop(1, peers, step, 0)
        mine = pl.ds(pl.multiple_of(me * 8, 8), 8)
        dst[mine, :] = src[mine, :]

    def arrive(src, dst, sems_s, sems_r):
        def step(i, carry):
            other = lax.rem(me + i, peers)
            carry_over(src, dst, sems_s, sems_r, other, other).wait_recv()
            return carry

        lax.fori_loop(1, peers, step, 0)

    def sent(src, dst, sems_s, sems_r):
        def step(i, carry):
            other = lax.rem(me + i, peers)
            carry_over(src, dst, sems_s, sems_r, other, me).wait_send()
            return carry

        lax.fori_loop(1, peers, step, 0)

    pl.semaphore_wait(barrier, peers - 1)
    exchange(send, recv, send1, recv1)

    def properties(z, carry):
        low, high = carry
        kind = soil[z]
        k = jnp.zeros((size_x, size_y), F32)
        a = k
        f = k
        for c in range(classes):
            hit = kind == c
            k = jnp.where(hit, ks_t[c], k)
            a = jnp.where(hit, al_t[c], a)
            f = jnp.where(hit, po_t[c], f)
        p = press[z]
        r = relperm(p, a)
        ks[z] = k
        al[z] = a
        phi[z] = f
        kr[z] = r
        for n, value in enumerate((p, k, r)):
            own_x[0, pl.ds(n * 16 + z, 1), :] = value[:1, :]
            own_x[1, pl.ds(n * 16 + z, 1), :] = value[size_x - 1 :, :]
            here = lane_id == n * 32 + z
            low = jnp.where(here, value[:, :1], low)
            high = jnp.where(here, value[:, size_y - 1 :], high)
        return low, high

    for n in (5, 0, 1, 2, 3):
        loads[n].wait()
    blank = jnp.zeros((size_x, size_y), F32)
    low, high = lax.fori_loop(0, depth, properties, (blank, blank))
    own_y[0] = low
    own_y[1] = high

    def sides(src_x, dst_x, src_y, dst_y, sems_s, sems_r):
        plan = (
            (my_x > 0, src_x, dst_x, 0, my_x - 1, my_y),
            (my_x < count_x - 1, src_x, dst_x, 1, my_x + 1, my_y),
            (my_y > 0, src_y, dst_y, 0, my_x, my_y - 1),
            (my_y < count_y - 1, src_y, dst_y, 1, my_x, my_y + 1),
        )
        made = []
        for n, (there, src, dst, side, at_x, at_y) in enumerate(plan):
            mate = n - side + 1 - side
            outward = pltpu.make_async_remote_copy(
                src_ref=src.at[side], dst_ref=dst.at[1 - side],
                send_sem=sems_s.at[n], recv_sem=sems_r.at[mate],
                device_id=(at_x, at_y), device_id_type=MESH,
            )
            inward = pltpu.make_async_remote_copy(
                src_ref=src.at[side], dst_ref=dst.at[side],
                send_sem=sems_s.at[n], recv_sem=sems_r.at[n],
                device_id=(at_x, at_y), device_id_type=MESH,
            )
            made.append((there, outward, inward))
        return made

    first_sides = sides(own_x, halo_x, own_y, halo_y, hs1, hr1)
    for there, outward, _ in first_sides:
        pl.when(there)(outward.start)

    def spread(j, carry):
        lanes = pl.ds(pl.multiple_of(j * 128, 128), 128)
        for src, dst in ((theta, th_s), (kappa, ka_s)):
            for k in range(0, levels, 8):
                n = min(8, levels - k)
                dst[pl.ds(k * rows + j, n, stride=rows), :] = src[k : k + n, lanes]
        return carry

    for n in (11, 12, 4):
        loads[n].wait()
    lax.fori_loop(0, rows, spread, 0, unroll=8)

    def outflow(z, before_z, pr, rel):
        p = pr[z]
        r = rel[z]
        zn = jnp.minimum(z + 1, depth - 1)
        fx = gx[z] * (r + pltpu.roll(r, 1, 0)) * (p - pltpu.roll(p, 1, 0))
        fy = gy[z] * (r + pltpu.roll(r, 1, 1)) * (p - pltpu.roll(p, 1, 1))
        down = gz[z] * (r + rel[zn]) * (p - pr[zn] + 1.0)
        total = (
            fx - pltpu.roll(fx, size_x - 1, 0) + fy - pltpu.roll(fy, size_y - 1, 1) + down - before_z
        )
        return total, down

    def boundary(z):
        total = jnp.where(row_id == 0, fbx[0, pl.ds(z, 1), :], 0.0)
        total = jnp.where(row_id == size_x - 1, fbx[1, pl.ds(z, 1), :], total)
        one = pltpu.roll(fby[0], lax.rem(size_y - z, size_y), 1)
        two = pltpu.roll(fby[1], size_y - 1 - z, 1)
        return total + jnp.where(lane_id == 0, one, 0.0) + jnp.where(lane_id == size_y - 1, two, 0.0)

    def faces(z, carry):
        k = ks[z]
        zn = jnp.minimum(z + 1, depth - 1)
        gx[z] = jnp.where(row_id == 0, 0.0, half_mean(k, pltpu.roll(k, 1, 0)))
        gy[z] = jnp.where(lane_id == 0, 0.0, half_mean(k, pltpu.roll(k, 1, 1)))
        gz[z] = jnp.where(z < depth - 1, half_mean(k, ks[zn]), 0.0)
        total, down = outflow(z, carry, press, kr)
        base[z] = press[z] - 0.8 * (phi[z] * (jnp.sqrt(kr[z]) - sat_old[z]) + 0.5 * total)
        return down

    lax.fori_loop(0, depth, faces, blank)

    for there, _, inward in first_sides:
        pl.when(there)(inward.wait_recv)
    for s in range(2):
        mine, other = own_x[s], halo_x[s]
        gbx[s] = half_mean(mine[16:32], other[16:32])
        fbx[s] = gbx[s] * (mine[32:48] + other[32:48]) * (mine[0:16] - other[0:16])
        mine, other = own_y[s], halo_y[s]
        gby[s] = half_mean(pltpu.roll(mine, size_y - 32, 1), pltpu.roll(other, size_y - 32, 1))
        fby[s] = gby[s] * pltpu.roll(mine + other, size_y - 64, 1) * (mine - other)

    arrive(send, recv, send1, recv1)
    macc[...] = jnp.zeros_like(macc)
    x_id = iota((size_x, 128), 0).astype(F32)
    x16 = iota16(size_x)
    y16 = iota16(size_y)
    srcs = GROUP // parts

    def gather_in(c, carry):
        lanes = pl.ds(pl.multiple_of(c * GROUP * 128, 128), GROUP * 128)
        left = [[] for _ in range(4)]
        right = []
        for i in range(srcs):
            got = recv[pl.ds(pl.multiple_of((c * srcs + i) * 8, 8), 8), :]
            high_v, low_v = halves(got)
            at_x = jnp.floor(got * (1.0 / size_y))
            at_y = got - at_x * size_y
            for h in range(parts):
                n = 2 * parts + h
                hit = wide_row(at_x[n : n + 1, :], size_x) == x16
                one = jnp.ones((size_y, 128), BF16)
                nothing = jnp.zeros((size_x, 128), BF16)
                right.append(
                    jnp.where(wide_row(at_y[n : n + 1, :], size_y) == y16, one, jnp.zeros_like(one))
                )
                for v in range(2):
                    m = v * parts + h
                    high_row = wide_row(high_v[m : m + 1, :], size_x)
                    low_row = wide_row(low_v[m : m + 1, :], size_x)
                    left[2 * v].append(jnp.where(hit, high_row, nothing))
                    left[2 * v + 1].append(jnp.where(hit, low_row, nothing))
        right = jnp.concatenate(right, axis=1)
        oney[:, lanes] = right
        left = jnp.concatenate([jnp.concatenate(l, axis=1) for l in left], axis=0)
        macc[...] += dot(left, right, NT)
        return carry

    lax.fori_loop(0, peers * parts // GROUP, gather_in, 0, unroll=4)
    rain_map = macc[0:size_x] + macc[size_x : 2 * size_x]
    et_map = macc[2 * size_x : 3 * size_x] + macc[3 * size_x : 4 * size_x]

    scale = 1.0 / sum(math.exp(-z / 2.0) for z in range(depth))

    def update(z, carry):
        frac, low, high = carry
        source = jnp.where(z == 0, rain_map, 0.0) - frac * et_map
        p = base[z] - 0.4 * boundary(z) + 0.4 * source
        r = relperm(p, al[z])
        p_out[z] = p
        krn[z] = r
        for n, value in enumerate((p, r)):
            own2_x[0, pl.ds(n * 16 + z, 1), :] = value[:1, :]
            own2_x[1, pl.ds(n * 16 + z, 1), :] = value[size_x - 1 :, :]
            here = lane_id == n * 32 + z
            low = jnp.where(here, value[:, :1], low)
            high = jnp.where(here, value[:, size_y - 1 :], high)
        return frac * math.exp(-0.5), low, high

    _, low, high = lax.fori_loop(0, depth, update, (jnp.float32(scale), blank, blank))
    own2_y[0] = low
    own2_y[1] = high
    second_sides = sides(own2_x, halo2_x, own2_y, halo2_y, hs2, hr2)
    for there, outward, _ in second_sides:
        pl.when(there)(outward.start)

    fields = []
    for field in (p_out[0], jnp.sqrt(krn[0])):
        high_v, low_v = halves(field)
        fields.append(jnp.concatenate([high_v, low_v], axis=1))
    top_s[...] = jnp.concatenate(fields, axis=0).astype(BF16)

    def answer(c, carry):
        lanes = pl.ds(pl.multiple_of(c * GROUP * 128, 128), GROUP * 128)
        right = oney[:, lanes]
        picked = dot(top_s[...], jnp.concatenate([right, right], axis=0), NN)
        for i in range(srcs):
            at = pl.ds(pl.multiple_of((c * srcs + i) * 8, 8), 8)
            at_x = jnp.floor(recv[at, :] * (1.0 / size_y))
            out = [None] * (2 * parts)
            for h in range(parts):
                n = 2 * parts + h
                hit = at_x[n : n + 1, :] == x_id
                j = (i * parts + h) * 128
                for v in range(2):
                    out[v * parts + h] = jnp.sum(
                        jnp.where(hit, picked[v * size_x : (v + 1) * size_x, j : j + 128], 0.0),
                        axis=0, keepdims=True,
                    )
            out.append(jnp.zeros((8 - 2 * parts, 128), F32))
            ans[at, :] = jnp.concatenate(out, axis=0)
        return carry

    lax.fori_loop(0, peers * parts // GROUP, answer, 0, unroll=4)
    exchange(ans, ret, send2, recv2)

    for there, _, inward in second_sides:
        pl.when(there)(inward.wait_recv)
    for s in range(2):
        mine, other = own2_x[s], halo2_x[s]
        fbx[s] = gbx[s] * (mine[16:32] + other[16:32]) * (mine[0:16] - other[0:16])
        mine, other = own2_y[s], halo2_y[s]
        fby[s] = gby[s] * pltpu.roll(mine + other, size_y - 32, 1) * (mine - other)

    def residual(z, carry):
        frac, previous = carry
        total, down = outflow(z, previous, p_out, krn)
        source = jnp.where(z == 0, rain_map, 0.0) - frac * et_map
        r_out[z] = phi[z] * (jnp.sqrt(krn[z]) - sat_old[z]) + 0.5 * (total + boundary(z)) - 0.5 * source
        return frac * math.exp(-0.5), down

    lax.fori_loop(0, depth, residual, (jnp.float32(scale), blank))

    arrive(ans, ret, send2, recv2)
    tops = []
    for v in range(2):
        value = jnp.concatenate(
            [ret[pl.ds(v * parts + h, peers, stride=8), :] for h in range(parts)], axis=1
        )
        tops.extend(halves(value))
    tops = jnp.concatenate(tops, axis=0).astype(BF16)

    def pick(c, carry):
        at = pl.ds(pl.multiple_of(c * GROUP, GROUP), GROUP)
        lanes = pl.ds(pl.multiple_of(c * GROUP * 128, 128), GROUP * 128)
        label = tile[at, :].astype(F32)
        picked = dot(tops, onehot[:, lanes], NN)
        for v in range(2):
            value = picked[2 * v * peers : (2 * v + 1) * peers]
            value = value + picked[(2 * v + 1) * peers : (2 * v + 2) * peers]
            found[v, at, :] = jnp.concatenate(
                [
                    jnp.sum(
                        jnp.where(label[i : i + 1, :] == peer_id, value[:, i * 128 : (i + 1) * 128], 0.0),
                        axis=0, keepdims=True,
                    )
                    for i in range(GROUP)
                ],
                axis=0,
            )
        return carry

    lax.fori_loop(0, rows // GROUP, pick, 0, unroll=4)

    many = 4 * GROUP

    def solve(c, carry):
        at = pl.ds(pl.multiple_of(c * many, many), many)
        ats = [pl.ds(pl.multiple_of(k * rows + c * many, GROUP), many) for k in range(levels)]
        p_top, s_top = found[0, at, :], found[1, at, :]
        active = mask[at, :] == 1
        coeff = [ka_s[ats[k], :] * (0.5 + s_top) for k in range(levels)]
        coeff.append(jnp.zeros_like(p_top))
        upper, value = [], []
        for k in range(levels):
            diag = 1.0 + coeff[k] + coeff[k + 1]
            right = th_s[ats[k], :]
            if k == 0:
                right = right + coeff[0] * p_top
            else:
                diag = diag - coeff[k] * upper[-1]
                right = right + coeff[k] * value[-1]
            inverse = 1.0 / diag
            upper.append(coeff[k + 1] * inverse)
            value.append(right * inverse)
        result = value[-1]
        so_s[ats[levels - 1], :] = jnp.where(active, result, th_s[ats[levels - 1], :])
        for k in range(levels - 2, -1, -1):
            result = value[k] + upper[k] * result
            so_s[ats[k], :] = jnp.where(active, result, th_s[ats[k], :])
        return carry

    lax.fori_loop(0, rows // many, solve, 0)

    def collect(j, carry):
        lanes = pl.ds(pl.multiple_of(j * 128, 128), 128)
        for k in range(0, levels, 8):
            n = min(8, levels - k)
            t_out[k : k + n, lanes] = so_s[pl.ds(k * rows + j, n, stride=rows), :]
        return carry

    lax.fori_loop(0, rows, collect, 0, unroll=8)

    sent(send, recv, send1, recv1)
    sent(ans, ret, send2, recv2)
    for made in (first_sides, second_sides):
        for there, outward, _ in made:
            pl.when(there)(outward.wait_send)


def write_out(*refs):
    done = refs[6]
    copies = [pltpu.make_async_copy(refs[n], refs[n + 3], done.at[n]) for n in range(3)]
    for copy in copies:
        copy.start()
    for copy in copies:
        copy.wait()


def local(dims, pressure, sat_old, soil_type, ks_table, alpha_table, porosity_table,
          rain, evapo, land_mask, tile, cell, theta, kappa):
    count_x, count_y = dims
    peers = count_x * count_y
    depth, size_x, size_y = pressure.shape
    levels, land = theta.shape
    slots = land // 32
    rows = land // 128
    flat = lambda value: value.reshape(rows, 128)
    grid = pltpu.VMEM((depth, size_x, size_y), F32)
    column = pltpu.VMEM((levels * rows, 128), F32)
    message = pltpu.VMEM((peers * 8, 128), F32)
    dma = pltpu.SemaphoreType.DMA
    vmem = pl.BlockSpec(memory_space=pltpu.VMEM)
    edge_x = pltpu.VMEM((2, 48, size_y), F32)
    edge2_x = pltpu.VMEM((2, 32, size_y), F32)
    edge_y = pltpu.VMEM((2, size_x, size_y), F32)
    rows_x = pltpu.VMEM((2, 16, size_y), F32)
    args = (
        ks_table, alpha_table, porosity_table, pressure, sat_old, soil_type,
        flat(rain), flat(evapo), flat(land_mask), flat(tile), flat(cell), theta, kappa,
    )
    held = [pltpu.SMEM(a.shape, a.dtype) for a in args[:3]]
    held += [pltpu.VMEM(a.shape, a.dtype) for a in args[3:]]
    hbm = pl.BlockSpec(memory_space=pltpu.HBM)
    outs = pl.pallas_call(
        functools.partial(kernel, (count_x, count_y, slots)),
        out_shape=(
            pltpu.VMEM(pressure.shape, F32),
            pltpu.VMEM(pressure.shape, F32),
            pltpu.VMEM(theta.shape, F32),
        ),
        in_specs=[hbm] * len(args),
        out_specs=(vmem, vmem, vmem),
        scratch_shapes=[
            *held,
            pltpu.VMEM((slots, land), BF16),
            pltpu.VMEM((6 * peers, slots), F32),
            message, message, message, message,
            grid, grid, grid, grid, grid, grid, grid, grid, grid,
            pltpu.VMEM((size_y, peers * slots), BF16),
            pltpu.VMEM((4 * size_x, size_y), F32),
            edge_x, edge_x, edge_y, edge_y, edge2_x, edge2_x, edge_y, edge_y,
            rows_x, edge_y, rows_x, edge_y,
            column, column, column,
            pltpu.VMEM((2 * size_x, 2 * size_y), BF16),
            pltpu.VMEM((2, rows, 128), F32),
            dma((peers,)), dma((peers,)), dma((peers,)), dma((peers,)),
            dma((4,)), dma((4,)), dma((4,)), dma((4,)), dma((len(args),)),
        ],
        compiler_params=pltpu.CompilerParams(
            collective_id=0, has_side_effects=True, vmem_limit_bytes=60 * 1024 * 1024
        ),
    )(*args)
    return pl.pallas_call(
        write_out,
        out_shape=tuple(jax.ShapeDtypeStruct(o.shape, F32) for o in outs),
        in_specs=[vmem] * 3,
        out_specs=(hbm, hbm, hbm),
        scratch_shapes=[dma((3,))],
        compiler_params=pltpu.CompilerParams(vmem_limit_bytes=8 * 1024 * 1024),
    )(*outs)


def solution(mesh):
    in_specs = (
        P(None, "gx", "gy"),
        P(None, "gx", "gy"),
        P(None, "gx", "gy"),
        P(),
        P(),
        P(),
        P(("gx", "gy")),
        P(("gx", "gy")),
        P(("gx", "gy")),
        P(("gx", "gy"), None),
        P(("gx", "gy")),
        P(None, ("gx", "gy")),
        P(None, ("gx", "gy")),
    )
    out_specs = (P(None, "gx", "gy"), P(None, "gx", "gy"), P(None, ("gx", "gy")))
    dims = (mesh.shape["gx"], mesh.shape["gy"])
    return jax.shard_map(
        functools.partial(local, dims), mesh=mesh, in_specs=in_specs, out_specs=out_specs, check_vma=False
    )
```

```python
import functools
import math

import jax
import jax.numpy as jnp
from jax import lax
from jax.experimental import pallas as pl
from jax.experimental.pallas import tpu as pltpu
from jax.sharding import PartitionSpec as P

F32 = jnp.float32
BF16 = jnp.bfloat16
MESH = pl.DeviceIdType.MESH
NT = (((1,), (1,)), ((), ()))
NN = (((1,), (0,)), ((), ()))
GROUP = 8


def dot(a, b, dims):
    return lax.dot_general(a, b, dims, preferred_element_type=F32)


def halves(value):
    high = value.astype(BF16).astype(F32)
    return high, value - high


def relperm(p, alpha):
    head = alpha * jnp.maximum(-p, 0.0)
    return 1.0 / (1.0 + head * head)


def half_mean(first, second):
    product = first * second
    total = first + second
    return jnp.where(product > 0, product / jnp.where(total > 0, total, 1.0), 0.0)


def wide_row(row, count):
    return jnp.concatenate([jnp.broadcast_to(row, (16, 128)).astype(BF16)] * (count // 16), axis=0)


def iota16(count):
    return lax.broadcasted_iota(jnp.int32, (count, 128), 0).astype(F32).astype(BF16)


def iota(shape, dim):
    return lax.broadcasted_iota(jnp.int32, shape, dim)


def kernel(
    dims,
    *refs,
):
    given, refs = refs[:13], refs[13:]
    (p_out, r_out, t_out), refs = refs[:3], refs[3:]
    held, refs = refs[:13], refs[13:]
    (ks_t, al_t, po_t, press, sat_old, soil, rain, evapo, mask, tile, cell, theta, kappa) = held
    (
        onehot, acc, send, recv, ans, ret,
        ks, al, phi, kr, gx, gy, gz, base, krn, oney, macc,
        own_x, halo_x, own_y, halo_y, own2_x, halo2_x, own2_y, halo2_y, gbx, gby, fbx, fby,
        th_s, ka_s, so_s, top_s, found,
        send1, recv1, send2, recv2, hs1, hr1, hs2, hr2, loaded,
    ) = refs
    loads = [
        pltpu.make_async_copy(src, dst, loaded.at[n]) for n, (src, dst) in enumerate(zip(given, held))
    ]
    for n in (9, 8, 10, 6, 7, 5, 0, 1, 2, 3, 4, 11, 12):
        loads[n].start()

    count_x, count_y, slots = dims
    peers = count_x * count_y
    depth, size_x, size_y = press.shape
    levels, land = theta.shape
    rows = land // 128
    parts = slots // 128
    classes = ks_t.shape[0]
    my_x = lax.axis_index("gx")
    my_y = lax.axis_index("gy")
    me = my_x * count_y + my_y

    for ref in (own_x, halo_x, own_y, halo_y, own2_x, halo2_x, own2_y, halo2_y):
        ref[...] = jnp.zeros_like(ref)

    barrier = pltpu.get_barrier_semaphore()

    def greet(i, carry):
        other = lax.rem(me + i, peers)
        pl.semaphore_signal(
            barrier, inc=1, device_id=(other // count_y, lax.rem(other, count_y)), device_id_type=MESH
        )
        return carry

    lax.fori_loop(1, peers, greet, 0)

    row_id = iota((size_x, size_y), 0)
    lane_id = iota((size_x, size_y), 1)

    wide = iota((128, 256), 1)
    tall = iota((128, 256), 0)
    before = ((wide >= 128) | (tall < wide)).astype(F32).astype(BF16)
    peer_id = iota((peers, 128), 0).astype(F32)
    peer16 = iota16(peers)
    slot16 = iota16(slots)
    acc[...] = jnp.zeros_like(acc)
    for n in (9, 8, 10, 6, 7):
        loads[n].wait()

    def dispatch(c, count):
        at = pl.ds(pl.multiple_of(c * GROUP, GROUP), GROUP)
        lanes = pl.ds(pl.multiple_of(c * GROUP * 128, 128), GROUP * 128)
        named = tile[at, :]
        live = mask[at, :].astype(F32)
        where_to = cell[at, :].astype(F32)
        cell_x = jnp.floor(where_to * (1.0 / size_y)) * size_y
        values = (
            *halves(live * rain[at, :]), *halves(live * evapo[at, :]), cell_x, where_to - cell_x
        )
        label = named.astype(F32)
        hits = [label[i : i + 1, :] == peer_id for i in range(GROUP)]
        hits16 = [wide_row(label[i : i + 1, :], peers) == peer16 for i in range(GROUP)]
        one = jnp.ones((peers, 128), BF16)
        sums = dot(
            jnp.concatenate([jnp.where(h, one, jnp.zeros_like(one)) for h in hits16], axis=0), before, NN
        )
        ranks = []
        for i in range(GROUP):
            part = sums[i * peers : (i + 1) * peers]
            ranks.append(
                jnp.sum(jnp.where(hits[i], part[:, :128] + count, 0.0), axis=0, keepdims=True)
            )
            count = count + part[:, 128:]
        one = jnp.ones((slots, 128), BF16)
        chosen = jnp.concatenate(
            [jnp.where(wide_row(r, slots) == slot16, one, jnp.zeros_like(one)) for r in ranks], axis=1
        )
        onehot[:, lanes] = chosen
        nothing = jnp.zeros((peers, 128), BF16)
        left = jnp.concatenate(
            [
                jnp.concatenate(
                    [
                        jnp.where(hits16[i], wide_row(v[i : i + 1, :], peers), nothing)
                        for i in range(GROUP)
                    ],
                    axis=1,
                )
                for v in values
            ],
            axis=0,
        )
        acc[...] += dot(left, chosen, NT)
        return count

    lax.fori_loop(0, rows // GROUP, dispatch, jnp.zeros((peers, 128), F32), unroll=4)
    for v in range(3):
        full = acc[2 * v * peers : (2 * v + 1) * peers] + acc[(2 * v + 1) * peers : (2 * v + 2) * peers]
        for h in range(parts):
            send[pl.ds(v * parts + h, peers, stride=8), :] = full[:, h * 128 : (h + 1) * 128]

    def block(ref, t):
        return ref.at[pl.ds(pl.multiple_of(t * 8, 8), 8)]

    def carry_over(src, dst, sems_s, sems_r, other, landing):
        return pltpu.make_async_remote_copy(
            src_ref=block(src, other), dst_ref=block(dst, landing),
            send_sem=sems_s, recv_sem=sems_r,
            device_id=(other // count_y, lax.rem(other, count_y)), device_id_type=MESH,
        )

    def exchange(src, dst, sems_s, sems_r):
        def step(i, carry):
            other = lax.rem(me + i, peers)
            carry_over(src, dst, sems_s, sems_r, other, me).start()
            return carry

        lax.fori_loop(1, peers, step, 0)
        mine = pl.ds(pl.multiple_of(me * 8, 8), 8)
        dst[mine, :] = src[mine, :]

    def everything(src, dst, sems_s, sems_r):
        most = pl.ds(0, (peers - 1) * 8)
        other = lax.rem(me + 1, peers)
        return pltpu.make_async_remote_copy(
            src_ref=src.at[most], dst_ref=dst.at[most], send_sem=sems_s, recv_sem=sems_r,
            device_id=(other // count_y, lax.rem(other, count_y)), device_id_type=MESH,
        )

    def arrive(*way):
        everything(*way).wait_recv()

    def sent(*way):
        everything(*way).wait_send()

    pl.semaphore_wait(barrier, peers - 1)
    exchange(send, recv, send1, recv1)

    def properties(z, carry):
        low, high = carry
        kind = soil[z]
        k = jnp.zeros((size_x, size_y), F32)
        a = k
        f = k
        for c in range(classes):
            hit = kind == c
            k = jnp.where(hit, ks_t[c], k)
            a = jnp.where(hit, al_t[c], a)
            f = jnp.where(hit, po_t[c], f)
        p = press[z]
        r = relperm(p, a)
        ks[z] = k
        al[z] = a
        phi[z] = f
        kr[z] = r
        for n, value in enumerate((p, k, r)):
            own_x[0, pl.ds(n * 16 + z, 1), :] = value[:1, :]
            own_x[1, pl.ds(n * 16 + z, 1), :] = value[size_x - 1 :, :]
            here = lane_id == n * 32 + z
            low = jnp.where(here, value[:, :1], low)
            high = jnp.where(here, value[:, size_y - 1 :], high)
        return low, high

    for n in (5, 0, 1, 2, 3):
        loads[n].wait()
    blank = jnp.zeros((size_x, size_y), F32)
    low, high = lax.fori_loop(0, depth, properties, (blank, blank))
    own_y[0] = low
    own_y[1] = high

    def sides(src_x, dst_x, src_y, dst_y, sems_s, sems_r):
        plan = (
            (my_x > 0, src_x, dst_x, 0, my_x - 1, my_y),
            (my_x < count_x - 1, src_x, dst_x, 1, my_x + 1, my_y),
            (my_y > 0, src_y, dst_y, 0, my_x, my_y - 1),
            (my_y < count_y - 1, src_y, dst_y, 1, my_x, my_y + 1),
        )
        made = []
        for n, (there, src, dst, side, at_x, at_y) in enumerate(plan):
            mate = n - side + 1 - side
            outward = pltpu.make_async_remote_copy(
                src_ref=src.at[side], dst_ref=dst.at[1 - side],
                send_sem=sems_s.at[n], recv_sem=sems_r.at[mate],
                device_id=(at_x, at_y), device_id_type=MESH,
            )
            inward = pltpu.make_async_remote_copy(
                src_ref=src.at[side], dst_ref=dst.at[side],
                send_sem=sems_s.at[n], recv_sem=sems_r.at[n],
                device_id=(at_x, at_y), device_id_type=MESH,
            )
            made.append((there, outward, inward))
        return made

    first_sides = sides(own_x, halo_x, own_y, halo_y, hs1, hr1)
    for there, outward, _ in first_sides:
        pl.when(there)(outward.start)

    def spread(j, carry):
        lanes = pl.ds(pl.multiple_of(j * 128, 128), 128)
        for src, dst in ((theta, th_s), (kappa, ka_s)):
            for k in range(0, levels, 8):
                n = min(8, levels - k)
                dst[pl.ds(k * rows + j, n, stride=rows), :] = src[k : k + n, lanes]
        return carry

    for n in (11, 12, 4):
        loads[n].wait()
    lax.fori_loop(0, rows, spread, 0, unroll=8)

    def outflow(z, before_z, pr, rel):
        p = pr[z]
        r = rel[z]
        zn = jnp.minimum(z + 1, depth - 1)
        fx = gx[z] * (r + pltpu.roll(r, 1, 0)) * (p - pltpu.roll(p, 1, 0))
        fy = gy[z] * (r + pltpu.roll(r, 1, 1)) * (p - pltpu.roll(p, 1, 1))
        down = gz[z] * (r + rel[zn]) * (p - pr[zn] + 1.0)
        total = (
            fx - pltpu.roll(fx, size_x - 1, 0) + fy - pltpu.roll(fy, size_y - 1, 1) + down - before_z
        )
        return total, down

    def boundary(z):
        total = jnp.where(row_id == 0, fbx[0, pl.ds(z, 1), :], 0.0)
        total = jnp.where(row_id == size_x - 1, fbx[1, pl.ds(z, 1), :], total)
        one = pltpu.roll(fby[0], lax.rem(size_y - z, size_y), 1)
        two = pltpu.roll(fby[1], size_y - 1 - z, 1)
        return total + jnp.where(lane_id == 0, one, 0.0) + jnp.where(lane_id == size_y - 1, two, 0.0)

    def faces(z, carry):
        k = ks[z]
        zn = jnp.minimum(z + 1, depth - 1)
        gx[z] = jnp.where(row_id == 0, 0.0, half_mean(k, pltpu.roll(k, 1, 0)))
        gy[z] = jnp.where(lane_id == 0, 0.0, half_mean(k, pltpu.roll(k, 1, 1)))
        gz[z] = jnp.where(z < depth - 1, half_mean(k, ks[zn]), 0.0)
        total, down = outflow(z, carry, press, kr)
        base[z] = press[z] - 0.8 * (phi[z] * (jnp.sqrt(kr[z]) - sat_old[z]) + 0.5 * total)
        return down

    lax.fori_loop(0, depth, faces, blank)

    for there, _, inward in first_sides:
        pl.when(there)(inward.wait_recv)
    for s in range(2):
        mine, other = own_x[s], halo_x[s]
        gbx[s] = half_mean(mine[16:32], other[16:32])
        fbx[s] = gbx[s] * (mine[32:48] + other[32:48]) * (mine[0:16] - other[0:16])
        mine, other = own_y[s], halo_y[s]
        gby[s] = half_mean(pltpu.roll(mine, size_y - 32, 1), pltpu.roll(other, size_y - 32, 1))
        fby[s] = gby[s] * pltpu.roll(mine + other, size_y - 64, 1) * (mine - other)

    arrive(send, recv, send1, recv1)
    macc[...] = jnp.zeros_like(macc)
    x_id = iota((size_x, 128), 0).astype(F32)
    x16 = iota16(size_x)
    y16 = iota16(size_y)
    srcs = GROUP // parts

    def gather_in(c, carry):
        lanes = pl.ds(pl.multiple_of(c * GROUP * 128, 128), GROUP * 128)
        left = [[] for _ in range(4)]
        right = []
        for i in range(srcs):
            got = recv[pl.ds(pl.multiple_of((c * srcs + i) * 8, 8), 8), :]
            high_v, low_v = halves(got)
            at_x = jnp.floor(got * (1.0 / size_y))
            at_y = got - at_x * size_y
            for h in range(parts):
                n = 2 * parts + h
                hit = wide_row(at_x[n : n + 1, :], size_x) == x16
                one = jnp.ones((size_y, 128), BF16)
                nothing = jnp.zeros((size_x, 128), BF16)
                right.append(
                    jnp.where(wide_row(at_y[n : n + 1, :], size_y) == y16, one, jnp.zeros_like(one))
                )
                for v in range(2):
                    m = v * parts + h
                    high_row = wide_row(high_v[m : m + 1, :], size_x)
                    low_row = wide_row(low_v[m : m + 1, :], size_x)
                    left[2 * v].append(jnp.where(hit, high_row, nothing))
                    left[2 * v + 1].append(jnp.where(hit, low_row, nothing))
        right = jnp.concatenate(right, axis=1)
        oney[:, lanes] = right
        left = jnp.concatenate([jnp.concatenate(l, axis=1) for l in left], axis=0)
        macc[...] += dot(left, right, NT)
        return carry

    lax.fori_loop(0, peers * parts // GROUP, gather_in, 0, unroll=4)
    rain_map = macc[0:size_x] + macc[size_x : 2 * size_x]
    et_map = macc[2 * size_x : 3 * size_x] + macc[3 * size_x : 4 * size_x]

    scale = 1.0 / sum(math.exp(-z / 2.0) for z in range(depth))

    def update(z, carry):
        frac, low, high = carry
        source = jnp.where(z == 0, rain_map, 0.0) - frac * et_map
        p = base[z] - 0.4 * boundary(z) + 0.4 * source
        r = relperm(p, al[z])
        p_out[z] = p
        krn[z] = r
        for n, value in enumerate((p, r)):
            own2_x[0, pl.ds(n * 16 + z, 1), :] = value[:1, :]
            own2_x[1, pl.ds(n * 16 + z, 1), :] = value[size_x - 1 :, :]
            here = lane_id == n * 32 + z
            low = jnp.where(here, value[:, :1], low)
            high = jnp.where(here, value[:, size_y - 1 :], high)
        return frac * math.exp(-0.5), low, high

    _, low, high = lax.fori_loop(0, depth, update, (jnp.float32(scale), blank, blank))
    own2_y[0] = low
    own2_y[1] = high
    second_sides = sides(own2_x, halo2_x, own2_y, halo2_y, hs2, hr2)
    for there, outward, _ in second_sides:
        pl.when(there)(outward.start)

    fields = []
    for field in (p_out[0], jnp.sqrt(krn[0])):
        high_v, low_v = halves(field)
        fields.append(jnp.concatenate([high_v, low_v], axis=1))
    top_s[...] = jnp.concatenate(fields, axis=0).astype(BF16)

    def answer(c, carry):
        others = [lax.rem(me + c * srcs + i + 1, peers) for i in range(srcs)]
        right = jnp.concatenate(
            [oney[:, pl.ds(pl.multiple_of(o * slots, slots), slots)] for o in others], axis=1
        )
        picked = dot(top_s[...], jnp.concatenate([right, right], axis=0), NN)
        for i, other in enumerate(others):
            at = pl.ds(pl.multiple_of(other * 8, 8), 8)
            at_x = jnp.floor(recv[at, :] * (1.0 / size_y))
            out = [None] * (2 * parts)
            for h in range(parts):
                n = 2 * parts + h
                hit = at_x[n : n + 1, :] == x_id
                j = (i * parts + h) * 128
                for v in range(2):
                    out[v * parts + h] = jnp.sum(
                        jnp.where(hit, picked[v * size_x : (v + 1) * size_x, j : j + 128], 0.0),
                        axis=0, keepdims=True,
                    )
            out.append(jnp.zeros((8 - 2 * parts, 128), F32))
            ans[at, :] = jnp.concatenate(out, axis=0)
        for other in others[: srcs - 1]:
            carry_over(ans, ret, send2, recv2, other, me).start()
        return carry

    turns = peers // srcs
    lax.fori_loop(0, turns, answer, 0, unroll=4)

    def rest(c, carry):
        other = lax.rem(me + (c + 1) * srcs, peers)
        carry_over(ans, ret, send2, recv2, other, me).start()
        return carry

    lax.fori_loop(0, turns - 1, rest, 0)
    mine = pl.ds(pl.multiple_of(me * 8, 8), 8)
    ret[mine, :] = ans[mine, :]

    for there, _, inward in second_sides:
        pl.when(there)(inward.wait_recv)
    for s in range(2):
        mine, other = own2_x[s], halo2_x[s]
        fbx[s] = gbx[s] * (mine[16:32] + other[16:32]) * (mine[0:16] - other[0:16])
        mine, other = own2_y[s], halo2_y[s]
        fby[s] = gby[s] * pltpu.roll(mine + other, size_y - 32, 1) * (mine - other)

    def residual(z, carry):
        frac, previous = carry
        total, down = outflow(z, previous, p_out, krn)
        source = jnp.where(z == 0, rain_map, 0.0) - frac * et_map
        r_out[z] = phi[z] * (jnp.sqrt(krn[z]) - sat_old[z]) + 0.5 * (total + boundary(z)) - 0.5 * source
        return frac * math.exp(-0.5), down

    lax.fori_loop(0, depth, residual, (jnp.float32(scale), blank))

    arrive(ans, ret, send2, recv2)
    tops = []
    for v in range(2):
        value = jnp.concatenate(
            [ret[pl.ds(v * parts + h, peers, stride=8), :] for h in range(parts)], axis=1
        )
        tops.extend(halves(value))
    tops = jnp.concatenate(tops, axis=0).astype(BF16)

    def pick(c, carry):
        at = pl.ds(pl.multiple_of(c * GROUP, GROUP), GROUP)
        lanes = pl.ds(pl.multiple_of(c * GROUP * 128, 128), GROUP * 128)
        label = tile[at, :].astype(F32)
        picked = dot(tops, onehot[:, lanes], NN)
        for v in range(2):
            value = picked[2 * v * peers : (2 * v + 1) * peers]
            value = value + picked[(2 * v + 1) * peers : (2 * v + 2) * peers]
            found[v, at, :] = jnp.concatenate(
                [
                    jnp.sum(
                        jnp.where(label[i : i + 1, :] == peer_id, value[:, i * 128 : (i + 1) * 128], 0.0),
                        axis=0, keepdims=True,
                    )
                    for i in range(GROUP)
                ],
                axis=0,
            )
        return carry

    lax.fori_loop(0, rows // GROUP, pick, 0, unroll=4)

    many = 4 * GROUP

    def solve(c, carry):
        at = pl.ds(pl.multiple_of(c * many, many), many)
        ats = [pl.ds(pl.multiple_of(k * rows + c * many, GROUP), many) for k in range(levels)]
        p_top, s_top = found[0, at, :], found[1, at, :]
        active = mask[at, :] == 1
        coeff = [ka_s[ats[k], :] * (0.5 + s_top) for k in range(levels)]
        coeff.append(jnp.zeros_like(p_top))
        upper, value = [], []
        for k in range(levels):
            diag = 1.0 + coeff[k] + coeff[k + 1]
            right = th_s[ats[k], :]
            if k == 0:
                right = right + coeff[0] * p_top
            else:
                diag = diag - coeff[k] * upper[-1]
                right = right + coeff[k] * value[-1]
            inverse = 1.0 / diag
            upper.append(coeff[k + 1] * inverse)
            value.append(right * inverse)
        result = value[-1]
        so_s[ats[levels - 1], :] = jnp.where(active, result, th_s[ats[levels - 1], :])
        for k in range(levels - 2, -1, -1):
            result = value[k] + upper[k] * result
            so_s[ats[k], :] = jnp.where(active, result, th_s[ats[k], :])
        return carry

    lax.fori_loop(0, rows // many, solve, 0)

    def collect(j, carry):
        lanes = pl.ds(pl.multiple_of(j * 128, 128), 128)
        for k in range(0, levels, 8):
            n = min(8, levels - k)
            t_out[k : k + n, lanes] = so_s[pl.ds(k * rows + j, n, stride=rows), :]
        return carry

    lax.fori_loop(0, rows, collect, 0, unroll=8)

    sent(send, recv, send1, recv1)
    sent(ans, ret, send2, recv2)
    for made in (first_sides, second_sides):
        for there, outward, _ in made:
            pl.when(there)(outward.wait_send)


def write_out(*refs):
    done = refs[6]
    copies = [pltpu.make_async_copy(refs[n], refs[n + 3], done.at[n]) for n in range(3)]
    for copy in copies:
        copy.start()
    for copy in copies:
        copy.wait()


def local(dims, pressure, sat_old, soil_type, ks_table, alpha_table, porosity_table,
          rain, evapo, land_mask, tile, cell, theta, kappa):
    count_x, count_y = dims
    peers = count_x * count_y
    depth, size_x, size_y = pressure.shape
    levels, land = theta.shape
    slots = land // 32
    rows = land // 128
    flat = lambda value: value.reshape(rows, 128)
    grid = pltpu.VMEM((depth, size_x, size_y), F32)
    column = pltpu.VMEM((levels * rows, 128), F32)
    message = pltpu.VMEM((peers * 8, 128), F32)
    dma = pltpu.SemaphoreType.DMA
    vmem = pl.BlockSpec(memory_space=pltpu.VMEM)
    edge_x = pltpu.VMEM((2, 48, size_y), F32)
    edge2_x = pltpu.VMEM((2, 32, size_y), F32)
    edge_y = pltpu.VMEM((2, size_x, size_y), F32)
    rows_x = pltpu.VMEM((2, 16, size_y), F32)
    args = (
        ks_table, alpha_table, porosity_table, pressure, sat_old, soil_type,
        flat(rain), flat(evapo), flat(land_mask), flat(tile), flat(cell), theta, kappa,
    )
    held = [pltpu.SMEM(a.shape, a.dtype) for a in args[:3]]
    held += [pltpu.VMEM(a.shape, a.dtype) for a in args[3:]]
    hbm = pl.BlockSpec(memory_space=pltpu.HBM)
    outs = pl.pallas_call(
        functools.partial(kernel, (count_x, count_y, slots)),
        out_shape=(
            pltpu.VMEM(pressure.shape, F32),
            pltpu.VMEM(pressure.shape, F32),
            pltpu.VMEM(theta.shape, F32),
        ),
        in_specs=[hbm] * len(args),
        out_specs=(vmem, vmem, vmem),
        scratch_shapes=[
            *held,
            pltpu.VMEM((slots, land), BF16),
            pltpu.VMEM((6 * peers, slots), F32),
            message, message, message, message,
            grid, grid, grid, grid, grid, grid, grid, grid, grid,
            pltpu.VMEM((size_y, peers * slots), BF16),
            pltpu.VMEM((4 * size_x, size_y), F32),
            edge_x, edge_x, edge_y, edge_y, edge2_x, edge2_x, edge_y, edge_y,
            rows_x, edge_y, rows_x, edge_y,
            column, column, column,
            pltpu.VMEM((2 * size_x, 2 * size_y), BF16),
            pltpu.VMEM((2, rows, 128), F32),
            dma, dma, dma, dma,
            dma((4,)), dma((4,)), dma((4,)), dma((4,)), dma((len(args),)),
        ],
        compiler_params=pltpu.CompilerParams(
            collective_id=0, has_side_effects=True, vmem_limit_bytes=60 * 1024 * 1024
        ),
    )(*args)
    return pl.pallas_call(
        write_out,
        out_shape=tuple(jax.ShapeDtypeStruct(o.shape, F32) for o in outs),
        in_specs=[vmem] * 3,
        out_specs=(hbm, hbm, hbm),
        scratch_shapes=[dma((3,))],
        compiler_params=pltpu.CompilerParams(vmem_limit_bytes=8 * 1024 * 1024),
    )(*outs)


def solution(mesh):
    in_specs = (
        P(None, "gx", "gy"),
        P(None, "gx", "gy"),
        P(None, "gx", "gy"),
        P(),
        P(),
        P(),
        P(("gx", "gy")),
        P(("gx", "gy")),
        P(("gx", "gy")),
        P(("gx", "gy"), None),
        P(("gx", "gy")),
        P(None, ("gx", "gy")),
        P(None, ("gx", "gy")),
    )
    out_specs = (P(None, "gx", "gy"), P(None, "gx", "gy"), P(None, ("gx", "gy")))
    dims = (mesh.shape["gx"], mesh.shape["gy"])
    return jax.shard_map(
        functools.partial(local, dims), mesh=mesh, in_specs=in_specs, out_specs=out_specs, check_vma=False
    )
```
